32 devices in a mesh: ang: 4 (over x, core), row: 8 (over z, y).
Axes of the slice: x: 2, y: 2, z: 4, core: 2. Of those that a mesh axis runs over, the one named last changes fastest.
Arguments:
- patches: bfloat16 [384, 2, 256, 256], P(('ang', 'row')), may hold values from -6 to 6
- owner: int32 [384], P(('ang', 'row')), may hold values from 0 to 7, as said below
- column: int32 [384], P(('ang', 'row')), may hold values from 0 to 1792
- angle_slot: int32 [384], P(('ang', 'row')), may hold values from 0 to 1
- probe: bfloat16 [2, 256, 256], replicated, may hold values from -1 to 1
- frames: bfloat16 [512, 256, 256], P(('ang', 'row')), may hold values from 0.099609375 to 3
- projection: bfloat16 [8, 2048, 2048], P('ang', 'row'), may hold values from -6 to 6
Outputs:
- refined_patches: bfloat16 [384, 2, 256, 256], P(('ang', 'row'))
- sinogram: bfloat16 [8, 8, 256, 2048], P(None, 'row', 'ang')
The draws below stay inside these ranges and needn't reach their ends.
Inputs may be any that keep to these rules, and one draw needn't show every extreme that they name: Among one device's 12 positions no owner appears more than 2 times; in every angle group one owner band receives exactly 2 positions from every device of the group.
All inputs are finite; a program needn't handle non-finite values.
Results may differ from the reference program's by a relative error of at most 0.0059.
Values may be sent and summed in bfloat16 or wider, within the bound.
A program may use at most 128 MiB of HBM per device.

```python
import math
import jax
import jax.numpy as jnp
from jax import lax

S = 256
W = 2048
ANG_DEV = 2
CAP = 2
PD = 12
ANGLES = 8
POSITIONS = 384
FRAMES = 512
N_ANG = 4
N_ROW = 8


def draw_owner(key, part):
    device_total = N_ANG * N_ROW
    base = jax.random.fold_in(key, 7)
    key_hot = jax.random.fold_in(base, 1)
    key_other = jax.random.fold_in(base, 2)
    key_shuffle = jax.random.fold_in(base, 3)
    hot_group = jax.random.randint(key_hot, (N_ANG,), 0, N_ROW)
    hot_device = jnp.repeat(hot_group, N_ROW)
    other_keys = jax.random.split(key_other, device_total)
    other_perm = jax.vmap(lambda single: jax.random.permutation(single, N_ROW - 1))(other_keys)
    picks = jnp.arange(PD - CAP, dtype=jnp.int32) % (N_ROW - 1)
    chosen = other_perm[:, picks]
    chosen = chosen + (chosen >= hot_device[:, None]).astype(jnp.int32)
    listed = jnp.concatenate([jnp.repeat(hot_device[:, None], CAP, axis=1), chosen], axis=1).astype(jnp.int32)
    shuffle_keys = jax.random.split(key_shuffle, device_total)
    shuffle = jax.vmap(lambda single: jax.random.permutation(single, PD))(shuffle_keys)
    result = jnp.take_along_axis(listed, shuffle, axis=1)
    return result.reshape(device_total * PD).astype(jnp.int32)


def with_ends(values, rng, least, high):
    shape = values.shape
    index_at = [jax.random.randint(jax.random.fold_in(rng, axis), (), 0, shape[axis]) for axis in range(len(shape))]
    values = values.at[tuple(index_at)].set(least)
    longest = shape.index(max(shape))
    index_at[longest] = (index_at[longest] + 1) % shape[longest]
    return values.at[tuple(index_at)].set(high)


def levels(own_key, shape, pieces, smallest, largest):
    def one(axis_at, blocks):
        steps = jax.random.uniform(jax.random.fold_in(jax.random.fold_in(own_key, 6), axis_at), (blocks,), jnp.float32, smallest / len(pieces), largest / len(pieces))
        return jnp.repeat(jnp.exp(steps), shape[axis_at] // blocks).reshape((-1,) + (1,) * (len(shape) - axis_at - 1))

    loudness = one(*pieces[0])
    for cut in pieces[1:]:
        loudness = loudness * one(*cut)
    return loudness


def normal_values(rng, shape, width, reach, cuts=(), kind=jnp.bfloat16):
    loudness = levels(rng, shape, cuts, -0.22, 0.18) if cuts else 1.0
    array = jax.random.normal(rng, shape, jnp.float32) * width * loudness
    return jnp.minimum(jnp.maximum(array, -reach), reach).astype(kind)


def setup_inputs(seed: int = 0) -> dict:
    splits = jax.random.split(jax.random.key(seed), 8)
    patches = normal_values(splits[0], (POSITIONS, 2, S, S), 1.0, 6.0, ((0, 32),))
    owner = draw_owner(jax.random.fold_in(splits[7], 71), 0)
    column = with_ends(jax.random.randint(splits[2], (POSITIONS,), 0, W - S + 1), jax.random.fold_in(splits[2], 1), 0, W - S).astype(jnp.int32)
    angle_slot = with_ends(jax.random.randint(splits[3], (POSITIONS,), 0, ANG_DEV), jax.random.fold_in(splits[3], 1), 0, ANG_DEV - 1).astype(jnp.int32)
    probe = jnp.clip(jax.random.uniform(splits[4], (2, S, S), jnp.float32, -1.0, 1.0), -1.0, 1.0).astype(jnp.bfloat16)
    frames = jnp.clip(jnp.exp(math.log(3.0) - 3.4051113 * jax.random.uniform(splits[5], (FRAMES, S, S), jnp.float32) ** levels(splits[5], (FRAMES, S, S), ((0, 32),), -0.2, 0.2)), 0.099609375, 3.0).astype(jnp.bfloat16)
    projection = normal_values(splits[6], (ANGLES, N_ROW * S, W), 1.0, 6.0, ((0, 4), (1, 8)))
    return {"patches": patches, "owner": owner, "column": column, "angle_slot": angle_slot, "probe": probe, "frames": frames, "projection": projection}


def dft_tables(size):
    positions = jnp.arange(size, dtype=jnp.int32)
    product = positions[:, None] * positions[None, :] % size
    phase = product.astype(jnp.float32) * (2.0 * math.pi / size)
    factor = 1.0 / math.sqrt(size)
    return ((jnp.cos(phase) * factor).astype(jnp.bfloat16), (-jnp.sin(phase) * factor).astype(jnp.bfloat16))

def matmul(left, right):
    return jnp.dot(left, right, preferred_element_type=jnp.float32)

def refine_one(patch, frame, probe, real_table, imag_table, scale_den):
    probe_real = probe[0].astype(jnp.float32)
    probe_imag = probe[1].astype(jnp.float32)
    object_real = patch[0].astype(jnp.float32)
    object_imag = patch[1].astype(jnp.float32)
    wave_real = (probe_real * object_real - probe_imag * object_imag).astype(jnp.bfloat16)
    wave_imag = (probe_real * object_imag + probe_imag * object_real).astype(jnp.bfloat16)
    first_real = (matmul(real_table, wave_real) - matmul(imag_table, wave_imag)).astype(jnp.bfloat16)
    first_imag = (matmul(real_table, wave_imag) + matmul(imag_table, wave_real)).astype(jnp.bfloat16)
    far_real = matmul(first_real, real_table) - matmul(first_imag, imag_table)
    far_imag = matmul(first_real, imag_table) + matmul(first_imag, real_table)
    magnitude = jnp.sqrt(far_real * far_real + far_imag * far_imag)
    factor = frame.astype(jnp.float32) / jnp.maximum(magnitude, 0.5)
    fixed_real = (factor * far_real).astype(jnp.bfloat16)
    fixed_imag = (factor * far_imag).astype(jnp.bfloat16)
    back_real = (matmul(real_table, fixed_real) + matmul(imag_table, fixed_imag)).astype(jnp.bfloat16)
    back_imag = (matmul(real_table, fixed_imag) - matmul(imag_table, fixed_real)).astype(jnp.bfloat16)
    near_real = matmul(back_real, real_table) + matmul(back_imag, imag_table)
    near_imag = matmul(back_imag, real_table) - matmul(back_real, imag_table)
    diff_real = near_real - wave_real.astype(jnp.float32)
    diff_imag = near_imag - wave_imag.astype(jnp.float32)
    step_real = probe_real * diff_real + probe_imag * diff_imag
    step_imag = probe_real * diff_imag - probe_imag * diff_real
    new_real = (object_real + step_real / scale_den).astype(jnp.bfloat16)
    new_imag = (object_imag + step_imag / scale_den).astype(jnp.bfloat16)
    return jnp.stack([new_real, new_imag])

def reference(patches, owner, column, angle_slot, probe, frames, projection):
    device_total = N_ANG * N_ROW
    owners = owner.reshape(device_total, PD)
    onehot = (owners[:, :, None] == jnp.arange(N_ROW, dtype=jnp.int32)[None, None, :]).astype(jnp.int32)
    order_rank = lax.optimization_barrier(jnp.sum((jnp.cumsum(onehot, axis=1) - onehot) * onehot, axis=2))
    device = jnp.arange(device_total, dtype=jnp.int32)[:, None]
    group_id = device // N_ROW
    band_id = device % N_ROW
    slot_index = (((group_id * N_ROW + owners) * N_ROW + band_id) * CAP + order_rank).reshape(POSITIONS).astype(jnp.int32)
    real_table, imag_table = dft_tables(S)
    probe_wide = probe.astype(jnp.float32)
    scale_den = jnp.max(probe_wide[0] * probe_wide[0] + probe_wide[1] * probe_wide[1]) + 1e-05

    def refine_position(pair_items):
        patch, slot_value = pair_items
        frame = lax.dynamic_index_in_dim(frames, slot_value, 0, keepdims=False)
        return refine_one(patch, frame, probe, real_table, imag_table, scale_den)
    refined_patches = lax.map(refine_position, (patches, slot_index))

    def place(position, accumulated):
        owner_device = position // PD
        angle_id = (owner_device // N_ROW * ANG_DEV + angle_slot[position]).astype(jnp.int32)
        row_start = (owner_device % N_ROW * S).astype(jnp.int32)
        col_start = column[position].astype(jnp.int32)
        tile_delta = refined_patches[position, 0].astype(jnp.float32) - patches[position, 0].astype(jnp.float32)
        current = lax.dynamic_slice(accumulated, (angle_id, row_start, col_start), (1, S, S))
        return lax.dynamic_update_slice(accumulated, current + tile_delta[None], (angle_id, row_start, col_start))
    accumulated = lax.fori_loop(0, POSITIONS, place, projection.astype(jnp.float32))
    sinogram = accumulated.astype(jnp.bfloat16).reshape(ANGLES, N_ROW, S, W)
    return (refined_patches, sinogram)
```

```python
import functools
import math

import jax
import jax.numpy as jnp
import ml_dtypes
import numpy as np
from jax import lax
from jax.experimental import pallas as pl
from jax.experimental.pallas import tpu as pltpu
from jax.sharding import PartitionSpec as P

MESH = pl.DeviceIdType.MESH
LANES = 128


def tables(size):
    position = np.arange(size)
    product = position[:, None] * position[None, :] % size
    phase = product.astype(np.float32) * np.float32(2.0 * math.pi / size)
    factor = np.float32(1.0 / math.sqrt(size))
    real = (np.cos(phase) * factor).astype(ml_dtypes.bfloat16)
    imag = (-np.sin(phase) * factor).astype(ml_dtypes.bfloat16)
    return np.block([[real, -imag], [imag, real]]), np.block([[real, imag], [-imag, real]])


def partner(me, step, count):
    result = 0
    bit = 1
    while bit < count:
        result = result + bit * lax.rem(lax.div(me, bit) + lax.div(step, bit), 2)
        bit *= 2
    return result


def i32(value):
    return jnp.int32(value)


def refine_kernel(
    n_a, n_r, capacity,
    owner_ref, column_ref, angle_ref, probe_ref, fwd_ref, inv_ref, patches, frames, projection,
    slots_out, delta_out, projection_out, info_out,
    held, frame_in, stage, delta, info,
    held_sem, own_sem, frame_send, frame_recv, stage_sem,
    delta_send, delta_recv, proj_send, proj_recv, info_send, info_recv,
):
    a, r = lax.axis_index("ang"), lax.axis_index("row")
    count, size = patches.shape[0], patches.shape[-1]
    slots = n_r * capacity
    rows = size // n_a

    barrier = pltpu.get_barrier_semaphore()
    for k in range(1, n_r):
        pl.semaphore_signal(
            barrier, inc=1, device_id=(a, partner(r, i32(k), n_r)), device_id_type=MESH
        )
    for j in range(1, n_a):
        pl.semaphore_signal(
            barrier, inc=1, device_id=(partner(a, i32(j), n_a), r), device_id_type=MESH
        )

    load = pltpu.make_async_copy(patches, held, held_sem)
    load.start()

    def own_frame(c):
        return pltpu.make_async_copy(
            frames.at[r * capacity + c], frame_in.at[c], own_sem.at[c]
        )

    def send_frame(s):
        step, c = lax.div(s, capacity), lax.rem(s, capacity)
        other = partner(r, step, n_r)
        return pltpu.make_async_remote_copy(
            src_ref=frames.at[other * capacity + c],
            dst_ref=frame_in.at[s],
            send_sem=frame_send.at[s],
            recv_sem=frame_recv.at[s],
            device_id=(a, other),
            device_id_type=MESH,
        )

    def send_projection(j):
        other = partner(a, i32(j), n_a)
        return pltpu.make_async_remote_copy(
            src_ref=projection.at[:, pl.ds(other * rows, rows), :],
            dst_ref=projection_out.at[j],
            send_sem=proj_send.at[j],
            recv_sem=proj_recv.at[j],
            device_id=(other, r),
            device_id_type=MESH,
        )

    def send_info(j):
        return pltpu.make_async_remote_copy(
            src_ref=info,
            dst_ref=info_out.at[j],
            send_sem=info_send.at[j],
            recv_sem=info_recv.at[j],
            device_id=(partner(a, i32(j), n_a), r),
            device_id_type=MESH,
        )

    def send_delta(j, s):
        other = partner(a, i32(j), n_a)
        return pltpu.make_async_remote_copy(
            src_ref=delta.at[s, pl.ds(other * rows, rows), :],
            dst_ref=delta_out.at[j, s],
            send_sem=delta_send.at[j, s],
            recv_sem=delta_recv.at[j, s],
            device_id=(other, r),
            device_id_type=MESH,
        )

    def own_delta(s):
        return pltpu.make_async_copy(
            delta.at[s, pl.ds(a * rows, rows), :], delta_out.at[0, s], delta_recv.at[0, s]
        )

    own_projection = pltpu.make_async_copy(
        projection.at[:, pl.ds(a * rows, rows), :], projection_out.at[0], proj_recv.at[0]
    )
    own_info = pltpu.make_async_copy(info, info_out.at[0], info_recv.at[0])

    for c in range(capacity):
        own_frame(c).start()

    owners = [owner_ref[p] for p in range(count)]
    row_id = lax.broadcasted_iota(jnp.int32, info.shape, 0)
    lane_id = lax.broadcasted_iota(jnp.int32, info.shape, 1)
    packed = jnp.zeros(info.shape, jnp.int32)
    for p in range(count):
        rank = i32(0)
        for q in range(p):
            rank = rank + jnp.where(owners[q] == owners[p], 1, 0)
        slot = partner(r, owners[p], n_r) * capacity + rank
        here = lane_id == p
        packed = jnp.where(here & (row_id == 0), slot, packed)
        packed = jnp.where(here & (row_id == 1), column_ref[p], packed)
        packed = jnp.where(here & (row_id == 2), angle_ref[p], packed)
    info[...] = packed

    pl.semaphore_wait(barrier, n_r - 1 + n_a - 1)

    def start_frames(i, carry):
        send_frame(slots - 1 - i).start()
        return carry

    lax.fori_loop(0, slots - capacity, start_frames, 0)
    for j in range(1, n_a):
        send_projection(j).start()
        send_info(j).start()
    own_projection.start()
    own_info.start()

    probe_real = probe_ref[0].astype(jnp.float32)
    probe_imag = probe_ref[1].astype(jnp.float32)
    peak = jnp.max(probe_real * probe_real + probe_imag * probe_imag)
    scale = 1.0 / (jnp.full((1, size), peak, jnp.float32) + 1e-05)

    load.wait()
    for c in range(capacity):
        own_frame(c).wait()

    def dot(left, right):
        return jnp.dot(left, right, preferred_element_type=jnp.float32)

    def one_slot(s, carry):
        owner = partner(r, lax.div(s, capacity), n_r)
        wanted = lax.rem(s, capacity)
        seen, position = i32(0), i32(0)
        for p in range(count):
            hit = owner_ref[p] == owner
            position = jnp.where(hit & (seen == wanted), i32(p), position)
            seen = seen + jnp.where(hit, 1, 0)

        pr = probe_ref[0].astype(jnp.float32)
        pi = probe_ref[1].astype(jnp.float32)
        patch_real = held[position, 0].astype(jnp.float32)
        patch_imag = held[position, 1].astype(jnp.float32)
        wave_real = (pr * patch_real - pi * patch_imag).astype(jnp.bfloat16)
        wave_imag = (pr * patch_imag + pi * patch_real).astype(jnp.bfloat16)
        first = dot(fwd_ref[...], jnp.concatenate([wave_real, wave_imag], axis=0))
        first = first.astype(jnp.bfloat16)
        far = dot(jnp.concatenate([first[:size], first[size:]], axis=1), inv_ref[...])
        far_real, far_imag = far[:, :size], far[:, size:]

        @pl.when(s >= capacity)
        def _():
            send_frame(s).wait_recv()

        power = jnp.maximum(far_real * far_real + far_imag * far_imag, 0.25)
        factor = frame_in[s].astype(jnp.float32) * lax.rsqrt(power)
        fixed_real = (factor * far_real).astype(jnp.bfloat16)
        fixed_imag = (factor * far_imag).astype(jnp.bfloat16)
        back = dot(inv_ref[...], jnp.concatenate([fixed_real, fixed_imag], axis=0))
        back = back.astype(jnp.bfloat16)
        near = dot(jnp.concatenate([back[:size], back[size:]], axis=1), fwd_ref[...])
        diff_real = near[:, :size] - wave_real.astype(jnp.float32)
        diff_imag = near[:, size:] - wave_imag.astype(jnp.float32)
        new_real = (patch_real + (pr * diff_real + pi * diff_imag) * scale).astype(jnp.bfloat16)
        new_imag = (patch_imag + (pr * diff_imag - pi * diff_real) * scale).astype(jnp.bfloat16)
        stage[s, 0] = new_real
        stage[s, 1] = new_imag
        delta[s] = (new_real.astype(jnp.float32) - patch_real).astype(jnp.bfloat16)
        for j in range(1, n_a):
            send_delta(j, s).start()
        own_delta(s).start()
        pltpu.make_async_copy(stage.at[s], slots_out.at[s], stage_sem.at[s]).start()
        return carry

    lax.fori_loop(0, slots, one_slot, 0)

    def finish(s, carry):
        @pl.when(s >= capacity)
        def _():
            send_frame(s).wait_send()

        for j in range(1, n_a):
            send_delta(j, s).wait_send()
            send_delta(j, s).wait_recv()
        own_delta(s).wait()
        pltpu.make_async_copy(stage.at[s], slots_out.at[s], stage_sem.at[s]).wait()
        return carry

    lax.fori_loop(0, slots, finish, 0)
    for j in range(1, n_a):
        send_projection(j).wait()
        send_info(j).wait()
    own_projection.wait()
    own_info.wait()


def place_kernel(
    angles, info_ref, projection_ref, delta_ref, slots_ref, sinogram_ref, refined_ref,
    total, sems,
):
    step = pl.program_id(0)
    last = pl.num_programs(0) - 1
    count = refined_ref.shape[0]
    rows, width = projection_ref.shape[2], projection_ref.shape[3]
    size = delta_ref.shape[-1]
    span = size + LANES

    def move(p):
        return pltpu.make_async_copy(
            slots_ref.at[info_ref[0, 0, p]], refined_ref.at[p], sems.at[p]
        )

    @pl.when(step == 0)
    def _():
        for p in range(count):
            move(p).start()

    for angle in range(angles):
        total[angle, :, :width] = projection_ref[0, angle].astype(jnp.float32)

    def place(p, carry):
        slot, column, angle = info_ref[step, 0, p], info_ref[step, 1, p], info_ref[step, 2, p]
        tile = lax.div(column, LANES)
        piece = delta_ref[0, slot].astype(jnp.float32)
        piece = jnp.concatenate([piece, jnp.zeros((rows, LANES), jnp.float32)], axis=1)
        piece = pltpu.roll(piece, lax.rem(column, LANES), 1)
        where = pl.ds(pl.multiple_of(tile * LANES, LANES), span)
        total[angle, :, where] += piece
        return carry

    lax.fori_loop(0, count, place, 0)
    for angle in range(angles):
        sinogram_ref[angle, 0] = total[angle, :, :width].astype(sinogram_ref.dtype)

    @pl.when(step == last)
    def _():
        for p in range(count):
            move(p).wait()


def local(n_a, n_r, patches, owner, column, angle_slot, probe, frames, projection):
    count, _, size, _ = patches.shape
    capacity = frames.shape[0] // n_r
    angles, _, width = projection.shape
    slots = n_r * capacity
    rows = size // n_a
    fwd, inv = tables(size)
    bf16 = jnp.bfloat16
    vmem = pl.BlockSpec(memory_space=pltpu.VMEM)
    smem = pl.BlockSpec(memory_space=pltpu.SMEM)
    hbm = pl.BlockSpec(memory_space=pl.ANY)
    dma = pltpu.SemaphoreType.DMA
    in_slots, deltas, projections, info = pl.pallas_call(
        functools.partial(refine_kernel, n_a, n_r, capacity),
        out_shape=(
            jax.ShapeDtypeStruct((slots, 2, size, size), bf16),
            jax.ShapeDtypeStruct((n_a, slots, rows, size), bf16),
            jax.ShapeDtypeStruct((n_a, angles, rows, width), bf16),
            jax.ShapeDtypeStruct((n_a, 8, LANES), jnp.int32),
        ),
        in_specs=[smem] * 3 + [vmem] * 3 + [hbm] * 3,
        out_specs=(hbm,) * 4,
        scratch_shapes=[
            pltpu.VMEM((count, 2, size, size), bf16),
            pltpu.VMEM((slots, size, size), bf16),
            pltpu.VMEM((slots, 2, size, size), bf16),
            pltpu.VMEM((slots, size, size), bf16),
            pltpu.VMEM((8, LANES), jnp.int32),
            dma,
            dma((capacity,)),
            dma((slots,)),
            dma((slots,)),
            dma((slots,)),
            dma((n_a, slots)),
            dma((n_a, slots)),
            dma((n_a,)),
            dma((n_a,)),
            dma((n_a,)),
            dma((n_a,)),
        ],
        compiler_params=pltpu.CompilerParams(
            collective_id=0, has_side_effects=True, vmem_limit_bytes=56 * 2**20
        ),
        name="refine",
    )(owner, column, angle_slot, probe, jnp.asarray(fwd), jnp.asarray(inv), patches, frames, projection)

    a = lax.axis_index("ang")
    mine = jnp.reshape(a, (1,)).astype(jnp.int32)

    def source(me, i):
        return partner(me, i, n_a)

    sinogram, refined = pl.pallas_call(
        functools.partial(placed, angles),
        grid_spec=pltpu.PrefetchScalarGridSpec(
            num_scalar_prefetch=1,
            grid=(n_a,),
            in_specs=[
                smem,
                pl.BlockSpec((1, angles, rows, width), lambda i, me: (i, 0, 0, 0)),
                pl.BlockSpec((1, slots, rows, size), lambda i, me: (i, 0, 0, 0)),
                hbm,
            ],
            out_specs=(
                pl.BlockSpec(
                    (angles, 1, rows, width), lambda i, me: (source(me[0], i), 0, 0, 0)
                ),
                hbm,
            ),
            scratch_shapes=[
                pltpu.VMEM((angles, rows, width + LANES), jnp.float32),
                dma((count,)),
            ],
        ),
        out_shape=(
            jax.ShapeDtypeStruct((n_a * angles, 1, rows, width), bf16),
            jax.ShapeDtypeStruct((count, 2, size, size), bf16),
        ),
        compiler_params=pltpu.CompilerParams(vmem_limit_bytes=32 * 2**20),
        name="place",
    )(mine, info, projections, deltas, in_slots)
    return refined, sinogram


def placed(angles, me_ref, *refs):
    place_kernel(angles, *refs)


def solution(mesh):
    return jax.shard_map(
        functools.partial(local, mesh.shape["ang"], mesh.shape["row"]),
        mesh=mesh,
        in_specs=(
            P(("ang", "row"), None, None, None),
            P(("ang", "row")),
            P(("ang", "row")),
            P(("ang", "row")),
            P(),
            P(("ang", "row"), None, None),
            P("ang", "row", None),
        ),
        out_specs=(P(("ang", "row"), None, None, None), P(None, "row", "ang", None)),
        check_vma=False,
    )
```

```python
import functools
import math

import jax
import jax.numpy as jnp
import ml_dtypes
import numpy as np
from jax import lax
from jax.experimental import pallas as pl
from jax.experimental.pallas import tpu as pltpu
from jax.sharding import PartitionSpec as P

MESH = pl.DeviceIdType.MESH
LANES = 128
WINDOW = 6


def tables(size):
    position = np.arange(size)
    product = position[:, None] * position[None, :] % size
    phase = product.astype(np.float32) * np.float32(2.0 * math.pi / size)
    factor = np.float32(1.0 / math.sqrt(size))
    real = (np.cos(phase) * factor).astype(ml_dtypes.bfloat16)
    imag = (-np.sin(phase) * factor).astype(ml_dtypes.bfloat16)
    return np.block([[real, -imag], [imag, real]]), np.block([[real, imag], [-imag, real]])


def partner(me, step, count):
    result = 0
    bit = 1
    while bit < count:
        result = result + bit * lax.rem(lax.div(me, bit) + lax.div(step, bit), 2)
        bit *= 2
    return result


def step_of(slot, capacity, count):
    turn = lax.div(slot, capacity)
    return lax.div(turn, 2) + lax.rem(turn, 2) * (count // 2)


def turn_of(step, count):
    return lax.rem(step, count // 2) * 2 + lax.div(step, count // 2)


def i32(value):
    return jnp.int32(value)


def refine_kernel(
    n_a, n_r, capacity,
    owner_ref, column_ref, angle_ref, probe_ref, fwd_ref, inv_ref, patches, frames, projection,
    slots_out, delta_out, projection_out, info_out,
    held, frame_in, stage, delta, info,
    held_sem, own_sem, frame_send, frame_recv, stage_sem,
    delta_send, delta_recv, proj_send, proj_recv, info_send, info_recv,
):
    a, r = lax.axis_index("ang"), lax.axis_index("row")
    count, size = patches.shape[0], patches.shape[-1]
    slots = n_r * capacity
    rows = size // n_a
    angles = projection.shape[0]

    barrier = pltpu.get_barrier_semaphore()
    for k in range(1, n_r):
        pl.semaphore_signal(
            barrier, inc=1, device_id=(a, partner(r, i32(k), n_r)), device_id_type=MESH
        )
    for j in range(1, n_a):
        pl.semaphore_signal(
            barrier, inc=1, device_id=(partner(a, i32(j), n_a), r), device_id_type=MESH
        )

    load = pltpu.make_async_copy(patches, held, held_sem)
    load.start()

    def own_frame(c):
        return pltpu.make_async_copy(
            frames.at[r * capacity + c], frame_in.at[c], own_sem.at[c]
        )

    def send_frame(s):
        c = lax.rem(s, capacity)
        other = partner(r, step_of(s, capacity, n_r), n_r)
        return pltpu.make_async_remote_copy(
            src_ref=frames.at[other * capacity + c],
            dst_ref=frame_in.at[s],
            send_sem=frame_send.at[s],
            recv_sem=frame_recv.at[s],
            device_id=(a, other),
            device_id_type=MESH,
        )

    def send_projection(j, angle):
        other = partner(a, i32(j), n_a)
        return pltpu.make_async_remote_copy(
            src_ref=projection.at[angle, pl.ds(other * rows, rows), :],
            dst_ref=projection_out.at[j, angle],
            send_sem=proj_send.at[j, angle],
            recv_sem=proj_recv.at[j, angle],
            device_id=(other, r),
            device_id_type=MESH,
        )

    def send_info(j):
        return pltpu.make_async_remote_copy(
            src_ref=info,
            dst_ref=info_out.at[j],
            send_sem=info_send.at[j],
            recv_sem=info_recv.at[j],
            device_id=(partner(a, i32(j), n_a), r),
            device_id_type=MESH,
        )

    def send_delta(j, s):
        other = partner(a, i32(j), n_a)
        return pltpu.make_async_remote_copy(
            src_ref=delta.at[s, pl.ds(other * rows, rows), :],
            dst_ref=delta_out.at[j, s],
            send_sem=delta_send.at[j, s],
            recv_sem=delta_recv.at[j, s],
            device_id=(other, r),
            device_id_type=MESH,
        )

    def own_delta(s):
        return pltpu.make_async_copy(
            delta.at[s, pl.ds(a * rows, rows), :], delta_out.at[0, s], delta_recv.at[0, s]
        )

    own_projection = pltpu.make_async_copy(
        projection.at[:, pl.ds(a * rows, rows), :], projection_out.at[0], proj_recv.at[0, 0]
    )
    own_info = pltpu.make_async_copy(info, info_out.at[0], info_recv.at[0])

    for c in range(capacity):
        own_frame(c).start()

    owners = [owner_ref[p] for p in range(count)]
    row_id = lax.broadcasted_iota(jnp.int32, info.shape, 0)
    lane_id = lax.broadcasted_iota(jnp.int32, info.shape, 1)
    packed = jnp.zeros(info.shape, jnp.int32)
    for p in range(count):
        rank = i32(0)
        for q in range(p):
            rank = rank + jnp.where(owners[q] == owners[p], 1, 0)
        slot = turn_of(partner(r, owners[p], n_r), n_r) * capacity + rank
        here = lane_id == p
        packed = jnp.where(here & (row_id == 0), slot, packed)
        packed = jnp.where(here & (row_id == 1), column_ref[p], packed)
        packed = jnp.where(here & (row_id == 2), angle_ref[p], packed)
    info[...] = packed

    pl.semaphore_wait(barrier, n_r - 1 + n_a - 1)

    window = min(WINDOW, slots - capacity)
    pieces = [(j, angle) for angle in range(angles) for j in range(n_a - 1, 0, -1)]
    for i in range(max(window, len(pieces))):
        if i < window:
            send_frame(i32(capacity + i)).start()
        if i < len(pieces):
            send_projection(*pieces[i]).start()
    for j in range(1, n_a):
        send_info(j).start()
    own_projection.start()
    own_info.start()

    probe_real = probe_ref[0].astype(jnp.float32)
    probe_imag = probe_ref[1].astype(jnp.float32)
    peak = jnp.max(probe_real * probe_real + probe_imag * probe_imag)
    scale = 1.0 / (jnp.full((1, size), peak, jnp.float32) + 1e-05)

    load.wait()
    for c in range(capacity):
        own_frame(c).wait()

    def dot(left, right):
        return jnp.dot(left, right, preferred_element_type=jnp.float32)

    def one_slot(s, carry):
        owner = partner(r, step_of(s, capacity, n_r), n_r)
        wanted = lax.rem(s, capacity)
        seen, position = i32(0), i32(0)
        for p in range(count):
            hit = owner_ref[p] == owner
            position = jnp.where(hit & (seen == wanted), i32(p), position)
            seen = seen + jnp.where(hit, 1, 0)

        pr = probe_ref[0].astype(jnp.float32)
        pi = probe_ref[1].astype(jnp.float32)
        patch_real = held[position, 0].astype(jnp.float32)
        patch_imag = held[position, 1].astype(jnp.float32)
        wave_real = (pr * patch_real - pi * patch_imag).astype(jnp.bfloat16)
        wave_imag = (pr * patch_imag + pi * patch_real).astype(jnp.bfloat16)
        first = dot(fwd_ref[...], jnp.concatenate([wave_real, wave_imag], axis=0))
        first = first.astype(jnp.bfloat16)
        far = dot(jnp.concatenate([first[:size], first[size:]], axis=1), inv_ref[...])
        far_real, far_imag = far[:, :size], far[:, size:]

        @pl.when(s >= capacity)
        def _():
            send_frame(s).wait_recv()

        @pl.when((s >= capacity) & (s + window < slots))
        def _():
            send_frame(s + window).start()

        power = jnp.maximum(far_real * far_real + far_imag * far_imag, 0.25)
        factor = frame_in[s].astype(jnp.float32) * lax.rsqrt(power)
        fixed_real = (factor * far_real).astype(jnp.bfloat16)
        fixed_imag = (factor * far_imag).astype(jnp.bfloat16)
        back = dot(inv_ref[...], jnp.concatenate([fixed_real, fixed_imag], axis=0))
        back = back.astype(jnp.bfloat16)
        near = dot(jnp.concatenate([back[:size], back[size:]], axis=1), fwd_ref[...])
        diff_real = near[:, :size] - wave_real.astype(jnp.float32)
        diff_imag = near[:, size:] - wave_imag.astype(jnp.float32)
        new_real = (patch_real + (pr * diff_real + pi * diff_imag) * scale).astype(jnp.bfloat16)
        new_imag = (patch_imag + (pr * diff_imag - pi * diff_real) * scale).astype(jnp.bfloat16)
        stage[s, 0] = new_real
        stage[s, 1] = new_imag
        delta[s] = (new_real.astype(jnp.float32) - patch_real).astype(jnp.bfloat16)
        for j in range(1, n_a):
            send_delta(j, s).start()
        own_delta(s).start()
        pltpu.make_async_copy(stage.at[s], slots_out.at[s], stage_sem.at[s]).start()
        return carry

    lax.fori_loop(0, slots, one_slot, 0)

    def finish(s, carry):
        @pl.when(s >= capacity)
        def _():
            send_frame(s).wait_send()

        for j in range(1, n_a):
            send_delta(j, s).wait_send()
            send_delta(j, s).wait_recv()
        own_delta(s).wait()
        pltpu.make_async_copy(stage.at[s], slots_out.at[s], stage_sem.at[s]).wait()
        return carry

    lax.fori_loop(0, slots, finish, 0)
    for j in range(1, n_a):
        for angle in range(angles):
            send_projection(j, angle).wait()
        send_info(j).wait()
    own_projection.wait()
    own_info.wait()


def place_kernel(
    angles, info_ref, projection_ref, delta_ref, slots_ref, sinogram_ref, refined_ref,
    total, bounce, in_sem, out_sem,
):
    step = pl.program_id(0)
    last = pl.num_programs(0) - 1
    count = refined_ref.shape[0]
    rows, width = projection_ref.shape[2], projection_ref.shape[3]
    size = delta_ref.shape[-1]
    span = size + LANES

    def fetch(p):
        return pltpu.make_async_copy(
            slots_ref.at[info_ref[0, 0, p]], bounce.at[p], in_sem.at[p]
        )

    def store(p):
        return pltpu.make_async_copy(bounce.at[p], refined_ref.at[p], out_sem.at[p])

    @pl.when(step == 0)
    def _():
        for p in range(count):
            fetch(p).start()

    for angle in range(angles):
        total[angle, :, :width] = projection_ref[0, angle].astype(jnp.float32)

    def place(p, carry):
        slot, column, angle = info_ref[step, 0, p], info_ref[step, 1, p], info_ref[step, 2, p]
        tile = lax.div(column, LANES)
        piece = delta_ref[0, slot].astype(jnp.float32)
        piece = jnp.concatenate([piece, jnp.zeros((rows, LANES), jnp.float32)], axis=1)
        piece = pltpu.roll(piece, lax.rem(column, LANES), 1)
        where = pl.ds(pl.multiple_of(tile * LANES, LANES), span)
        total[angle, :, where] += piece
        return carry

    lax.fori_loop(0, count, place, 0, unroll=True)
    @pl.when(step == 0)
    def _():
        for p in range(count):
            fetch(p).wait()
            store(p).start()

    for angle in range(angles):
        sinogram_ref[angle, 0] = total[angle, :, :width].astype(sinogram_ref.dtype)

    @pl.when(step == last)
    def _():
        for p in range(count):
            store(p).wait()


def local(n_a, n_r, patches, owner, column, angle_slot, probe, frames, projection):
    count, _, size, _ = patches.shape
    capacity = frames.shape[0] // n_r
    angles, _, width = projection.shape
    slots = n_r * capacity
    rows = size // n_a
    fwd, inv = tables(size)
    bf16 = jnp.bfloat16
    vmem = pl.BlockSpec(memory_space=pltpu.VMEM)
    smem = pl.BlockSpec(memory_space=pltpu.SMEM)
    hbm = pl.BlockSpec(memory_space=pl.ANY)
    dma = pltpu.SemaphoreType.DMA
    in_slots, deltas, projections, info = pl.pallas_call(
        functools.partial(refine_kernel, n_a, n_r, capacity),
        out_shape=(
            jax.ShapeDtypeStruct((slots, 2, size, size), bf16),
            jax.ShapeDtypeStruct((n_a, slots, rows, size), bf16),
            jax.ShapeDtypeStruct((n_a, angles, rows, width), bf16),
            jax.ShapeDtypeStruct((n_a, 8, LANES), jnp.int32),
        ),
        in_specs=[smem] * 3 + [vmem] * 3 + [hbm] * 3,
        out_specs=(hbm,) * 4,
        scratch_shapes=[
            pltpu.VMEM((count, 2, size, size), bf16),
            pltpu.VMEM((slots, size, size), bf16),
            pltpu.VMEM((slots, 2, size, size), bf16),
            pltpu.VMEM((slots, size, size), bf16),
            pltpu.VMEM((8, LANES), jnp.int32),
            dma,
            dma((capacity,)),
            dma((slots,)),
            dma((slots,)),
            dma((slots,)),
            dma((n_a, slots)),
            dma((n_a, slots)),
            dma((n_a, angles)),
            dma((n_a, angles)),
            dma((n_a,)),
            dma((n_a,)),
        ],
        compiler_params=pltpu.CompilerParams(
            collective_id=0, has_side_effects=True, vmem_limit_bytes=56 * 2**20
        ),
        name="refine",
    )(owner, column, angle_slot, probe, jnp.asarray(fwd), jnp.asarray(inv), patches, frames, projection)

    a = lax.axis_index("ang")
    mine = jnp.reshape(a, (1,)).astype(jnp.int32)

    def source(me, i):
        return partner(me, i, n_a)

    sinogram, refined = pl.pallas_call(
        functools.partial(placed, angles),
        grid_spec=pltpu.PrefetchScalarGridSpec(
            num_scalar_prefetch=1,
            grid=(n_a,),
            in_specs=[
                smem,
                pl.BlockSpec((1, angles, rows, width), lambda i, me: (i, 0, 0, 0)),
                pl.BlockSpec((1, slots, rows, size), lambda i, me: (i, 0, 0, 0)),
                hbm,
            ],
            out_specs=(
                pl.BlockSpec(
                    (angles, 1, rows, width), lambda i, me: (source(me[0], i), 0, 0, 0)
                ),
                hbm,
            ),
            scratch_shapes=[
                pltpu.VMEM((angles, rows, width + LANES), jnp.float32),
                pltpu.VMEM((count, 2, size, size), bf16),
                dma((count,)),
                dma((count,)),
            ],
        ),
        out_shape=(
            jax.ShapeDtypeStruct((n_a * angles, 1, rows, width), bf16),
            jax.ShapeDtypeStruct((count, 2, size, size), bf16),
        ),
        compiler_params=pltpu.CompilerParams(vmem_limit_bytes=60 * 2**20),
        name="place",
    )(mine, info, projections, deltas, in_slots)
    return refined, sinogram


def placed(angles, me_ref, *refs):
    place_kernel(angles, *refs)


def solution(mesh):
    return jax.shard_map(
        functools.partial(local, mesh.shape["ang"], mesh.shape["row"]),
        mesh=mesh,
        in_specs=(
            P(("ang", "row"), None, None, None),
            P(("ang", "row")),
            P(("ang", "row")),
            P(("ang", "row")),
            P(),
            P(("ang", "row"), None, None),
            P("ang", "row", None),
        ),
        out_specs=(P(("ang", "row"), None, None, None), P(None, "row", "ang", None)),
        check_vma=False,
    )
```

```python
import functools
import math

import jax
import jax.numpy as jnp
import ml_dtypes
import numpy as np
from jax import lax
from jax.experimental import pallas as pl
from jax.experimental.pallas import tpu as pltpu
from jax.sharding import PartitionSpec as P

MESH = pl.DeviceIdType.MESH
LANES = 128


def tables(size):
    position = np.arange(size)
    product = position[:, None] * position[None, :] % size
    phase = product.astype(np.float32) * np.float32(2.0 * math.pi / size)
    factor = np.float32(1.0 / math.sqrt(size))
    real = (np.cos(phase) * factor).astype(ml_dtypes.bfloat16)
    imag = (-np.sin(phase) * factor).astype(ml_dtypes.bfloat16)
    return np.block([[real, -imag], [imag, real]]), np.block([[real, imag], [-imag, real]])


def partner(me, step, count):
    result = 0
    bit = 1
    while bit < count:
        result = result + bit * lax.rem(lax.div(me, bit) + lax.div(step, bit), 2)
        bit *= 2
    return result


def step_of(slot, capacity, count):
    turn = lax.div(slot, capacity)
    return lax.div(turn, 2) + lax.rem(turn, 2) * (count // 2)


def turn_of(step, count):
    return lax.rem(step, count // 2) * 2 + lax.div(step, count // 2)


def i32(value):
    return jnp.int32(value)


def refine_kernel(
    n_a, n_r, capacity,
    owner_ref, column_ref, angle_ref, probe, fwd, inv, patches, frames, projection,
    slots_out, delta_out, projection_out, info_out,
    held, probe_ref, fwd_ref, inv_ref, far_ref, frame_in, stage, delta, info,
    held_sem, own_sem, frame_send, frame_recv, stage_sem,
    delta_send, delta_recv, proj_send, proj_recv, info_send, info_recv,
):
    a, r = lax.axis_index("ang"), lax.axis_index("row")
    count, size = patches.shape[0], patches.shape[-1]
    slots = n_r * capacity
    rows = size // n_a
    angles = projection.shape[0]

    barrier = pltpu.get_barrier_semaphore()
    for k in range(1, n_r):
        pl.semaphore_signal(
            barrier, inc=1, device_id=(a, partner(r, i32(k), n_r)), device_id_type=MESH
        )
    for j in range(1, n_a):
        pl.semaphore_signal(
            barrier, inc=1, device_id=(partner(a, i32(j), n_a), r), device_id_type=MESH
        )

    loads = [
        pltpu.make_async_copy(source, target, held_sem.at[i])
        for i, (source, target) in enumerate(
            [(probe, probe_ref), (fwd, fwd_ref), (inv, inv_ref), (patches, held)]
        )
    ]
    for load in loads:
        load.start()

    def own_frame(c):
        return pltpu.make_async_copy(
            frames.at[r * capacity + c], frame_in.at[c], own_sem.at[c]
        )

    def send_frame(s):
        c = lax.rem(s, capacity)
        other = partner(r, step_of(s, capacity, n_r), n_r)
        return pltpu.make_async_remote_copy(
            src_ref=frames.at[other * capacity + c],
            dst_ref=frame_in.at[s],
            send_sem=frame_send.at[s],
            recv_sem=frame_recv.at[s],
            device_id=(a, other),
            device_id_type=MESH,
        )

    def send_projection(j, angle):
        other = partner(a, i32(j), n_a)
        return pltpu.make_async_remote_copy(
            src_ref=projection.at[angle, pl.ds(other * rows, rows), :],
            dst_ref=projection_out.at[j, angle],
            send_sem=proj_send.at[j, angle],
            recv_sem=proj_recv.at[j, angle],
            device_id=(other, r),
            device_id_type=MESH,
        )

    def send_info(j):
        return pltpu.make_async_remote_copy(
            src_ref=info,
            dst_ref=info_out.at[j],
            send_sem=info_send.at[j],
            recv_sem=info_recv.at[j],
            device_id=(partner(a, i32(j), n_a), r),
            device_id_type=MESH,
        )

    def send_delta(j, s):
        other = partner(a, i32(j), n_a)
        return pltpu.make_async_remote_copy(
            src_ref=delta.at[s, pl.ds(other * rows, rows), :],
            dst_ref=delta_out.at[j, s],
            send_sem=delta_send.at[j, s],
            recv_sem=delta_recv.at[j, s],
            device_id=(other, r),
            device_id_type=MESH,
        )

    def own_delta(s):
        return pltpu.make_async_copy(
            delta.at[s, pl.ds(a * rows, rows), :], delta_out.at[0, s], delta_recv.at[0, s]
        )

    own_projection = pltpu.make_async_copy(
        projection.at[:, pl.ds(a * rows, rows), :], projection_out.at[0], proj_recv.at[0, 0]
    )
    own_info = pltpu.make_async_copy(info, info_out.at[0], info_recv.at[0])

    for c in range(capacity):
        own_frame(c).start()

    owners = [owner_ref[p] for p in range(count)]
    row_id = lax.broadcasted_iota(jnp.int32, info.shape, 0)
    lane_id = lax.broadcasted_iota(jnp.int32, info.shape, 1)
    packed = jnp.zeros(info.shape, jnp.int32)
    for p in range(count):
        rank = i32(0)
        for q in range(p):
            rank = rank + jnp.where(owners[q] == owners[p], 1, 0)
        slot = turn_of(partner(r, owners[p], n_r), n_r) * capacity + rank
        here = lane_id == p
        packed = jnp.where(here & (row_id == 0), slot, packed)
        packed = jnp.where(here & (row_id == 1), column_ref[p], packed)
        packed = jnp.where(here & (row_id == 2), angle_ref[p], packed)
    info[...] = packed

    pl.semaphore_wait(barrier, n_r - 1 + n_a - 1)

    window = slots - capacity
    pieces = [(j, angle) for angle in range(angles) for j in range(n_a - 1, 0, -1)]
    for i in range(max(window, len(pieces))):
        if i < window:
            send_frame(i32(capacity + i)).start()
        if i < len(pieces):
            send_projection(*pieces[i]).start()
    for j in range(1, n_a):
        send_info(j).start()
    own_projection.start()
    own_info.start()

    for load in loads:
        load.wait()
    probe_real = probe_ref[0].astype(jnp.float32)
    probe_imag = probe_ref[1].astype(jnp.float32)
    peak = jnp.max(probe_real * probe_real + probe_imag * probe_imag)
    scale = 1.0 / (jnp.full((1, size), peak, jnp.float32) + 1e-05)

    def dot(left, right):
        return jnp.dot(left, right, preferred_element_type=jnp.float32)

    def wave_of(position):
        pr = probe_ref[0].astype(jnp.float32)
        pi = probe_ref[1].astype(jnp.float32)
        patch_real = held[position, 0].astype(jnp.float32)
        patch_imag = held[position, 1].astype(jnp.float32)
        wave_real = (pr * patch_real - pi * patch_imag).astype(jnp.bfloat16)
        wave_imag = (pr * patch_imag + pi * patch_real).astype(jnp.bfloat16)
        return pr, pi, patch_real, patch_imag, wave_real, wave_imag

    def forward(p, carry):
        wave_real, wave_imag = wave_of(p)[-2:]
        first = dot(fwd_ref[...], jnp.concatenate([wave_real, wave_imag], axis=0))
        first = first.astype(jnp.bfloat16)
        far_ref[p] = dot(jnp.concatenate([first[:size], first[size:]], axis=1), inv_ref[...])
        return carry

    lax.fori_loop(0, count, forward, 0)
    for c in range(capacity):
        own_frame(c).wait()

    def one_slot(s, carry):
        owner = partner(r, step_of(s, capacity, n_r), n_r)
        wanted = lax.rem(s, capacity)
        seen, position = i32(0), i32(0)
        for p in range(count):
            hit = owner_ref[p] == owner
            position = jnp.where(hit & (seen == wanted), i32(p), position)
            seen = seen + jnp.where(hit, 1, 0)

        pr, pi, patch_real, patch_imag, wave_real, wave_imag = wave_of(position)
        far_real, far_imag = far_ref[position, :, :size], far_ref[position, :, size:]

        @pl.when(s >= capacity)
        def _():
            send_frame(s).wait_recv()

        power = jnp.maximum(far_real * far_real + far_imag * far_imag, 0.25)
        factor = frame_in[s].astype(jnp.float32) * lax.rsqrt(power)
        fixed_real = (factor * far_real).astype(jnp.bfloat16)
        fixed_imag = (factor * far_imag).astype(jnp.bfloat16)
        back = dot(inv_ref[...], jnp.concatenate([fixed_real, fixed_imag], axis=0))
        back = back.astype(jnp.bfloat16)
        near = dot(jnp.concatenate([back[:size], back[size:]], axis=1), fwd_ref[...])
        diff_real = near[:, :size] - wave_real.astype(jnp.float32)
        diff_imag = near[:, size:] - wave_imag.astype(jnp.float32)
        new_real = (patch_real + (pr * diff_real + pi * diff_imag) * scale).astype(jnp.bfloat16)
        new_imag = (patch_imag + (pr * diff_imag - pi * diff_real) * scale).astype(jnp.bfloat16)
        stage[s, 0] = new_real
        stage[s, 1] = new_imag
        delta[s] = (new_real.astype(jnp.float32) - patch_real).astype(jnp.bfloat16)
        for j in range(1, n_a):
            send_delta(j, s).start()
        own_delta(s).start()
        pltpu.make_async_copy(stage.at[s], slots_out.at[s], stage_sem.at[s]).start()
        return carry

    lax.fori_loop(0, slots, one_slot, 0)

    def finish(s, carry):
        @pl.when(s >= capacity)
        def _():
            send_frame(s).wait_send()

        for j in range(1, n_a):
            send_delta(j, s).wait_send()
            send_delta(j, s).wait_recv()
        own_delta(s).wait()
        pltpu.make_async_copy(stage.at[s], slots_out.at[s], stage_sem.at[s]).wait()
        return carry

    lax.fori_loop(0, slots, finish, 0)
    for j in range(1, n_a):
        for angle in range(angles):
            send_projection(j, angle).wait()
        send_info(j).wait()
    own_projection.wait()
    own_info.wait()


def place_kernel(
    angles, info_ref, projection_ref, delta_ref, slots_ref, sinogram_ref, refined_ref,
    total, bounce, in_sem, out_sem,
):
    step = pl.program_id(0)
    last = pl.num_programs(0) - 1
    count = refined_ref.shape[0]
    rows, width = projection_ref.shape[2], projection_ref.shape[3]
    size = delta_ref.shape[-1]
    span = size + LANES

    def fetch(p):
        return pltpu.make_async_copy(
            slots_ref.at[info_ref[0, 0, p]], bounce.at[p], in_sem.at[p]
        )

    def store(p):
        return pltpu.make_async_copy(bounce.at[p], refined_ref.at[p], out_sem.at[p])

    @pl.when(step == 0)
    def _():
        for p in range(count):
            fetch(p).start()

    for angle in range(angles):
        total[angle, :, :width] = projection_ref[0, angle].astype(jnp.float32)

    def place(p, carry):
        slot, column, angle = info_ref[step, 0, p], info_ref[step, 1, p], info_ref[step, 2, p]
        tile = lax.div(column, LANES)
        piece = delta_ref[0, slot].astype(jnp.float32)
        piece = jnp.concatenate([piece, jnp.zeros((rows, LANES), jnp.float32)], axis=1)
        piece = pltpu.roll(piece, lax.rem(column, LANES), 1)
        where = pl.ds(pl.multiple_of(tile * LANES, LANES), span)
        total[angle, :, where] += piece
        return carry

    lax.fori_loop(0, count, place, 0, unroll=True)
    @pl.when(step == 0)
    def _():
        for p in range(count):
            fetch(p).wait()
            store(p).start()

    for angle in range(angles):
        sinogram_ref[angle, 0] = total[angle, :, :width].astype(sinogram_ref.dtype)

    @pl.when(step == last)
    def _():
        for p in range(count):
            store(p).wait()


def local(n_a, n_r, patches, owner, column, angle_slot, probe, frames, projection):
    count, _, size, _ = patches.shape
    capacity = frames.shape[0] // n_r
    angles, _, width = projection.shape
    slots = n_r * capacity
    rows = size // n_a
    fwd, inv = tables(size)
    bf16 = jnp.bfloat16
    smem = pl.BlockSpec(memory_space=pltpu.SMEM)
    hbm = pl.BlockSpec(memory_space=pl.ANY)
    dma = pltpu.SemaphoreType.DMA
    in_slots, deltas, projections, info = pl.pallas_call(
        functools.partial(refine_kernel, n_a, n_r, capacity),
        out_shape=(
            jax.ShapeDtypeStruct((slots, 2, size, size), bf16),
            jax.ShapeDtypeStruct((n_a, slots, rows, size), bf16),
            jax.ShapeDtypeStruct((n_a, angles, rows, width), bf16),
            jax.ShapeDtypeStruct((n_a, 8, LANES), jnp.int32),
        ),
        in_specs=[smem] * 3 + [hbm] * 6,
        out_specs=(hbm,) * 4,
        scratch_shapes=[
            pltpu.VMEM((count, 2, size, size), bf16),
            pltpu.VMEM((2, size, size), bf16),
            pltpu.VMEM(fwd.shape, bf16),
            pltpu.VMEM(inv.shape, bf16),
            pltpu.VMEM((count, size, 2 * size), jnp.float32),
            pltpu.VMEM((slots, size, size), bf16),
            pltpu.VMEM((slots, 2, size, size), bf16),
            pltpu.VMEM((slots, size, size), bf16),
            pltpu.VMEM((8, LANES), jnp.int32),
            dma((4,)),
            dma((capacity,)),
            dma((slots,)),
            dma((slots,)),
            dma((slots,)),
            dma((n_a, slots)),
            dma((n_a, slots)),
            dma((n_a, angles)),
            dma((n_a, angles)),
            dma((n_a,)),
            dma((n_a,)),
        ],
        compiler_params=pltpu.CompilerParams(
            collective_id=0, has_side_effects=True, vmem_limit_bytes=56 * 2**20
        ),
        name="refine",
    )(owner, column, angle_slot, probe, jnp.asarray(fwd), jnp.asarray(inv), patches, frames, projection)

    a = lax.axis_index("ang")
    mine = jnp.reshape(a, (1,)).astype(jnp.int32)

    def source(me, i):
        return partner(me, i, n_a)

    sinogram, refined = pl.pallas_call(
        functools.partial(placed, angles),
        grid_spec=pltpu.PrefetchScalarGridSpec(
            num_scalar_prefetch=1,
            grid=(n_a,),
            in_specs=[
                smem,
                pl.BlockSpec((1, angles, rows, width), lambda i, me: (i, 0, 0, 0)),
                pl.BlockSpec((1, slots, rows, size), lambda i, me: (i, 0, 0, 0)),
                hbm,
            ],
            out_specs=(
                pl.BlockSpec(
                    (angles, 1, rows, width), lambda i, me: (source(me[0], i), 0, 0, 0)
                ),
                hbm,
            ),
            scratch_shapes=[
                pltpu.VMEM((angles, rows, width + LANES), jnp.float32),
                pltpu.VMEM((count, 2, size, size), bf16),
                dma((count,)),
                dma((count,)),
            ],
        ),
        out_shape=(
            jax.ShapeDtypeStruct((n_a * angles, 1, rows, width), bf16),
            jax.ShapeDtypeStruct((count, 2, size, size), bf16),
        ),
        compiler_params=pltpu.CompilerParams(vmem_limit_bytes=60 * 2**20),
        name="place",
    )(mine, info, projections, deltas, in_slots)
    return refined, sinogram


def placed(angles, me_ref, *refs):
    place_kernel(angles, *refs)


def solution(mesh):
    return jax.shard_map(
        functools.partial(local, mesh.shape["ang"], mesh.shape["row"]),
        mesh=mesh,
        in_specs=(
            P(("ang", "row"), None, None, None),
            P(("ang", "row")),
            P(("ang", "row")),
            P(("ang", "row")),
            P(),
            P(("ang", "row"), None, None),
            P("ang", "row", None),
        ),
        out_specs=(P(("ang", "row"), None, None, None), P(None, "row", "ang", None)),
        check_vma=False,
    )
```
